256 devices in a mesh: dp: 32 (over z, x), tensor: 8 (over y, core).
Axes of the slice: x: 4, y: 4, z: 8, core: 2. Of those that a mesh axis runs over, the one named last changes fastest.
Arguments:
- gate_grad: bfloat16 [32, 256, 14336], P('dp', None, 'tensor'), may hold values from -6 to 6
- up_grad: bfloat16 [32, 256, 14336], P('dp', None, 'tensor'), may hold values from -6 to 6
- gate_error: float32 [32, 256, 14336], P('dp', None, 'tensor'), may hold values from -4 to 4
- up_error: float32 [32, 256, 14336], P('dp', None, 'tensor'), may hold values from -4 to 4
- gate_q: float32 [14336, 32], P('tensor'), may hold values from -6 to 6
- up_q: float32 [14336, 32], P('tensor'), may hold values from -6 to 6
Outputs:
- gate_sum: bfloat16 [256, 14336], P(None, 'tensor')
- up_sum: bfloat16 [256, 14336], P(None, 'tensor')
- gate_next_q: float32 [14336, 32], P('tensor')
- up_next_q: float32 [14336, 32], P('tensor')
- gate_new_error: float32 [32, 256, 14336], P('dp', None, 'tensor')
- up_new_error: float32 [32, 256, 14336], P('dp', None, 'tensor')
The draws below stay inside these ranges and needn't reach their ends.
All inputs are finite; a program needn't handle non-finite values.
Results may differ from the reference program's by a relative error of at most 0.0011.
Values sent between devices are 32-bit elements; how exact they have to be, the bound alone decides.
A program may use at most 64 MiB of HBM per device.

```python
import jax
import jax.numpy as jnp
from jax import lax

FF = 14336
RANK = 32
ROWS = 256
REPL = 32


def shard_levels(own_key, extent, cuts, least, largest):
    level = 1.0
    for axis_at, blocks in cuts:
        steps = jax.random.uniform(jax.random.fold_in(jax.random.fold_in(own_key, 6), axis_at), (blocks,), jnp.float32, least / len(cuts), largest / len(cuts))
        level = level * jnp.repeat(jnp.exp(steps), extent[axis_at] // blocks).reshape((-1,) + (1,) * (len(extent) - 1 - axis_at))
    return level


def centred(rng, extent, width, most, split=(), dtype=jnp.bfloat16):
    entries = jax.random.normal(rng, extent, jnp.float32) * width
    if len(split) > 0:
        entries = shard_levels(rng, extent, split, -0.22, 0.18) * entries
    return jnp.clip(entries, min=-most, max=most).astype(dtype)


def setup_inputs(seed: int = 0) -> dict:
    splits = jax.random.split(jax.random.key(seed), 7)
    return {
        "gate_grad": centred(splits[0], (REPL, ROWS, FF), 1.0, 6.0, ((0, 32), (2, 8))),
        "up_grad": centred(splits[1], (REPL, ROWS, FF), 1.0, 6.0, ((0, 32), (2, 8))),
        "gate_error": centred(splits[2], (REPL, ROWS, FF), 0.5, 4.0, ((0, 32), (2, 8)), jnp.float32),
        "up_error": centred(splits[3], (REPL, ROWS, FF), 0.5, 4.0, ((0, 32), (2, 8)), jnp.float32),
        "gate_q": centred(splits[4], (FF, RANK), 1.0, 6.0, ((0, 8),), jnp.float32),
        "up_q": centred(splits[5], (FF, RANK), 1.0, 6.0, ((0, 8),), jnp.float32),
    }


def compress(grad, error, prev_q):
    full = grad.astype(jnp.float32) + error
    total = jnp.sum(full, axis=0)
    left = jnp.dot(total, prev_q, precision=lax.Precision.HIGHEST)
    gram = jnp.dot(left.T, left, precision=lax.Precision.HIGHEST)
    factor = jnp.linalg.cholesky(gram)
    ortho = lax.linalg.triangular_solve(factor, left, left_side=False, lower=True, transpose_a=True)
    own_q = jnp.einsum('kif,ir->kfr', full, ortho, precision=lax.Precision.HIGHEST)
    new_error = full - jnp.einsum('ir,kfr->kif', ortho, own_q, precision=lax.Precision.HIGHEST)
    next_q = jnp.sum(own_q, axis=0)
    summed = jnp.dot(ortho, next_q.T, precision=lax.Precision.HIGHEST).astype(jnp.bfloat16)
    return (summed, next_q, new_error)

def reference(gate_grad, up_grad, gate_error, up_error, gate_q, up_q):
    gate_sum, gate_next, gate_new = compress(gate_grad, gate_error, gate_q)
    up_sum, up_next, up_new = compress(up_grad, up_error, up_q)
    return (gate_sum, up_sum, gate_next, up_next, gate_new, up_new)
```

```python
import functools

import jax
import jax.numpy as jnp
from jax import lax
from jax.experimental import pallas as pl
from jax.experimental.pallas import tpu as pltpu
from jax.sharding import PartitionSpec as P

MESH = pl.DeviceIdType.MESH
F32, BF16 = jnp.float32, jnp.bfloat16
HIGHEST = lax.Precision.HIGHEST
NX, NY, NZ = 4, 4, 8
ROWS, RANK, WIDE = 256, 32, 1792
CH = 256
NCH = WIDE // CH
NN = (((1,), (0,)), ((), ()))
NT = (((1,), (1,)), ((), ()))
TN = (((0,), (0,)), ((), ()))


def split(value):
    high = value.astype(BF16)
    low = (value - high.astype(F32)).astype(BF16)
    return high, low


def product(a, b, dims):
    return lax.dot_general(a, b, dims, preferred_element_type=F32)


def inverse_factor(gram):
    row = lax.broadcasted_iota(jnp.int32, (RANK, RANK), 0)
    lane = lax.broadcasted_iota(jnp.int32, (RANK, RANK), 1)
    unit = jnp.where(row == lane, 1.0, 0.0).astype(F32)
    pivots = jnp.ones((RANK, RANK), F32)
    for j in range(RANK):
        column = jnp.broadcast_to(gram[:, j : j + 1], (RANK, RANK))
        pivot = jnp.broadcast_to(column[j : j + 1, :], (RANK, RANK))
        pivots = jnp.where(row == j, pivot, pivots)
        if j < RANK - 1:
            factor = jnp.where(row > j, column / pivot, 0.0)
            gram = gram - factor * gram[j : j + 1, :]
            unit = unit - factor * unit[j : j + 1, :]
    return unit * lax.rsqrt(pivots)


def main_kernel(
    grad0, grad1, error0, error1, q0, q1,
    sum0, sum1, next0, next1, new0, new1,
    graw, full, qv, fhi, flo, psend, precv, ybuf, zbuf, lmine, left,
    tbuf, xr, zs, zr, tsum, inv, wide,
    ldg, lde, ldq, s1, r1, s2, r2, s3, r3, s4, r4,
    sx, rx, sz, rz, sgz, rgz, sgx, rgx,
):
    grads, errors, qs = (grad0, grad1), (error0, error1), (q0, q1)
    sums, nexts, news = (sum0, sum1), (next0, next1), (new0, new1)
    dp, tensor = lax.axis_index("dp"), lax.axis_index("tensor")
    z, x, y, c = dp // NX, dp % NX, tensor // 2, tensor % 2

    def device(dz=0, dx=0, dy=0, dc=0):
        return (
            lax.rem(z + dz, NZ) * NX + lax.rem(x + dx, NX),
            lax.rem(y + dy, NY) * 2 + lax.rem(c + dc, 2),
        )

    def send(src, dst, send_sem, recv_sem, to):
        pltpu.make_async_remote_copy(
            src_ref=src, dst_ref=dst, send_sem=send_sem, recv_sem=recv_sem,
            device_id=to, device_id_type=MESH,
        ).start()

    def wait(ref, sem):
        pltpu.make_async_copy(ref, ref, sem).wait()

    for b in range(2):
        pltpu.make_async_copy(qs[b], qv.at[b], ldq.at[b]).start()
        for j in range(NCH):
            cols = pl.ds(j * CH, CH)
            pltpu.make_async_copy(errors[b].at[0, :, cols], full.at[b, j], lde.at[b, j]).start()
            pltpu.make_async_copy(grads[b].at[0, :, cols], graw.at[b, j], ldg.at[b, j]).start()

    barrier = pltpu.get_barrier_semaphore()
    xc = [(dx, dc) for dx in (2, 1, 3, 0) for dc in range(2) if (dx, dc) != (0, 0)]
    peers = [device(dx=dx, dc=dc) for dx, dc in xc]
    peers += [device(dy=k) for k in (2, 1, 3)]
    peers += [device(dz=k) for k in (4, 3, 5, 2, 6, 1, 7)]
    for peer in peers:
        pl.semaphore_signal(barrier, inc=1, device_id=peer, device_id_type=MESH)

    for b in range(2):
        wait(qv.at[b], ldq.at[b])
        qhi, qlo = split(qv[b])
        both = jnp.concatenate([qhi, qlo], axis=0)
        acc = jnp.zeros((RANK, ROWS), F32)
        for j in range(NCH):
            wait(full.at[b, j], lde.at[b, j])
            wait(graw.at[b, j], ldg.at[b, j])
            value = graw[b, j].astype(F32) + full[b, j]
            high, low = split(value)
            full[b, j], fhi[b, j], flo[b, j] = value, high, low
            cols = slice(j * CH, (j + 1) * CH)
            first = product(both[:, cols], high, NT)
            acc += first[:RANK] + first[RANK:] + product(qhi[:, cols], low, NT)
        for k in range(4):
            psend[4 * b + k] = acc[8 * k : 8 * k + 8]
        if b == 0:
            pl.semaphore_wait(barrier, len(peers))

    mine = c * NX + x
    for dx, dc in xc:
        there = lax.rem(c + dc, 2) * NX + lax.rem(x + dx, NX)
        send(psend.at[there], precv.at[dc * NX + dx - 1], s1, r1, device(dx=dx, dc=dc))
    wait(precv, r1)
    part = psend[mine]
    for k in range(7):
        part += precv[k]
    ybuf[0] = part
    for k in (2, 1, 3):
        send(ybuf.at[0], ybuf.at[k], s2, r2, device(dy=k))
    wait(ybuf.at[pl.ds(1, 3)], r2)
    part = ybuf[y]
    for k in range(1, NY):
        part += ybuf[lax.rem(y - k + NY, NY)]
    zbuf[0] = part
    for k in (4, 3, 5, 2, 6, 1, 7):
        send(zbuf.at[0], zbuf.at[k], s3, r3, device(dz=k))
    wait(zbuf.at[pl.ds(1, 7)], r3)
    part = zbuf[z]
    for k in range(1, NZ):
        part += zbuf[lax.rem(z - k + NZ, NZ)]
    lmine[...] = part
    for dx, dc in xc:
        send(lmine, left.at[mine], s4, r4.at[c], device(dx=dx, dc=dc))
    pltpu.make_async_copy(lmine, left.at[mine], r4.at[c]).start()

    lefts, lhs = [], []
    for b in range(2):
        wait(left.at[pl.ds(4 * b, 4)], r4.at[b])
        lefts.append(left[4 * b : 4 * b + 4].reshape(RANK, ROWS))
        lhi, llo = split(lefts[b])
        lhs.append((jnp.concatenate([lhi, llo], axis=0), lhi))
    chunks = [lax.rem(z + 3 + k, NCH) for k in range(NCH)]
    for chunk in chunks:
        for b in range(2):
            first = product(lhs[b][0], fhi[b, chunk], NN)
            value = first[:RANK] + first[RANK:] + product(lhs[b][1], flo[b, chunk], NN)
            tbuf[chunk, 2 * b] = value[:16]
            tbuf[chunk, 2 * b + 1] = value[16:]
        for dx in (2, 1, 3):
            send(
                tbuf.at[chunk, lax.rem(x + dx, NX)], xr.at[chunk, dx - 1], sx, rx.at[chunk], device(dx=dx)
            )

    for chunk in chunks:
        wait(xr.at[chunk], rx.at[chunk])
        zs[chunk] = tbuf[chunk, x] + xr[chunk, 0] + xr[chunk, 1] + xr[chunk, 2]

        @pl.when(chunk != z)
        def _():
            send(
                zs.at[chunk], zr.at[lax.rem(chunk - z + NZ, NZ)], sz.at[chunk], rz,
                device(dz=chunk - z + NZ),
            )

    for b in range(2):
        gram = lax.dot_general(lefts[b], lefts[b], NT, precision=HIGHEST, preferred_element_type=F32)
        inverse = inverse_factor(gram)
        ortho = lax.dot_general(inverse, lefts[b], NN, precision=HIGHEST, preferred_element_type=F32)
        weight = lax.dot_general(inverse, ortho, TN, precision=HIGHEST, preferred_element_type=F32)
        whi = weight.astype(BF16).astype(F32)
        wide[b] = jnp.concatenate([whi, whi, weight - whi], axis=0).T.astype(BF16)
        inv[b] = inverse

    @pl.when(z < NCH)
    def _():
        wait(zr.at[pl.ds(1, 7)], rz)
        part = zs[z]
        for k in range(1, NZ):
            part += zr[k]
        tsum[z, x] = part
        for k in (4, 3, 5, 2, 6, 1, 7):
            send(tsum.at[z, x], tsum.at[z, x], sgz, rgz.at[z], device(dz=k))
        for dx in (2, 1, 3):
            send(tsum.at[z, x], tsum.at[z, x], sgx, rgx.at[z, dx - 1], device(dx=dx))

    def triple(value):
        high, low = split(value)
        return jnp.concatenate([high, low, high], axis=0)

    for b in range(2):
        for j in range(NCH):
            own = tbuf[j, 2 * b : 2 * b + 2].reshape(RANK, CH)
            cols = slice(j * CH, (j + 1) * CH)
            news[b][:, cols] = full[b, j] - product(wide[b], triple(own), NN)

    for k in (1, 7, 2, 6, 3, 5, 4):
        at = lax.rem(z + k, NZ)

        @pl.when(at < NCH)
        def _():
            wait(tsum.at[at, x], rgz.at[at])
            for dx in (2, 1, 3):
                send(tsum.at[at, x], tsum.at[at, x], sgx, rgx.at[at, dx - 1], device(dx=dx))

    for k in (0, 1, 7, 2, 6, 3, 5, 4):
        at = lax.rem(z + k, NZ)

        @pl.when(at < NCH)
        def _():
            for dx in (1, 3, 2):
                wait(tsum.at[at, lax.rem(x - dx + NX, NX)], rgx.at[at, dx - 1])
            cols = pl.ds(pl.multiple_of(at * CH, CH), CH)
            for b in range(2):
                total = tsum[at, 2 * b : 2 * b + 2].reshape(RANK, CH)
                sums[b][:, cols] = product(wide[b], triple(total), NN).astype(BF16)
                nexts[b][:, cols] = lax.dot_general(
                    inv[b], total, NN, precision=HIGHEST, preferred_element_type=F32
                )

    wait(precv, s1)
    wait(ybuf.at[pl.ds(1, 3)], s2)
    wait(zbuf.at[pl.ds(1, 7)], s3)
    wait(precv, s4)
    wait(xr, sx)
    wait(xr, sgx)
    for k in range(NCH):

        @pl.when(k != z)
        def _():
            wait(zs.at[k], sz.at[k])

    @pl.when(z < NCH)
    def _():
        wait(zr.at[pl.ds(1, 7)], sgz)


def store_kernel(*refs):
    ins, outs, sem = refs[:6], refs[6:12], refs[12]
    copies = [pltpu.make_async_copy(a, b, sem.at[i]) for i, (a, b) in enumerate(zip(ins, outs))]
    for copy in copies:
        copy.start()
    for copy in copies:
        copy.wait()


def shards(grad0, grad1, error0, error1, q0, q1):
    vmem = pl.BlockSpec(memory_space=pltpu.VMEM)
    hbm = pl.BlockSpec(memory_space=pltpu.HBM)
    shapes = [
        ((ROWS, WIDE), BF16), ((ROWS, WIDE), BF16),
        ((RANK, WIDE), F32), ((RANK, WIDE), F32),
        ((ROWS, WIDE), F32), ((ROWS, WIDE), F32),
    ]
    dma = pltpu.SemaphoreType.DMA
    scratch = [
        pltpu.VMEM((2, NCH, ROWS, CH), BF16),
        pltpu.VMEM((2, NCH, ROWS, CH), F32),
        pltpu.VMEM((2, RANK, WIDE), F32),
        pltpu.VMEM((2, NCH, ROWS, CH), BF16),
        pltpu.VMEM((2, NCH, ROWS, CH), BF16),
        pltpu.VMEM((8, 8, ROWS), F32),
        pltpu.VMEM((7, 8, ROWS), F32),
        pltpu.VMEM((NY, 8, ROWS), F32),
        pltpu.VMEM((NZ, 8, ROWS), F32),
        pltpu.VMEM((8, ROWS), F32),
        pltpu.VMEM((8, 8, ROWS), F32),
        pltpu.VMEM((NCH, NX, 16, CH), F32),
        pltpu.VMEM((NCH, NX - 1, 16, CH), F32),
        pltpu.VMEM((NCH, 16, CH), F32),
        pltpu.VMEM((NZ, 16, CH), F32),
        pltpu.VMEM((NCH, NX, 16, CH), F32),
        pltpu.VMEM((2, RANK, RANK), F32),
        pltpu.VMEM((2, ROWS, 3 * RANK), BF16),
        dma((2, NCH)), dma((2, NCH)), dma((2,)),
        dma, dma, dma, dma, dma, dma, dma, dma((2,)),
        dma, dma((NCH,)), dma((NCH,)), dma,
        dma, dma((NCH,)), dma, dma((NCH, NX - 1)),
    ]
    held = pl.pallas_call(
        main_kernel,
        out_shape=[pltpu.VMEM(s, d) for s, d in shapes],
        in_specs=[hbm] * 6,
        out_specs=[vmem] * 6,
        scratch_shapes=scratch,
        name="compress",
        compiler_params=pltpu.CompilerParams(
            collective_id=0, has_side_effects=True, vmem_limit_bytes=36 << 20
        ),
    )(*[pltpu.with_memory_space_constraint(a, pltpu.HBM) for a in (grad0, grad1, error0, error1, q0.T, q1.T)])
    outs = pl.pallas_call(
        store_kernel,
        out_shape=[jax.ShapeDtypeStruct(s, d) for s, d in shapes],
        in_specs=[vmem] * 6,
        out_specs=[hbm] * 6,
        scratch_shapes=[dma((6,))],
        name="store",
        compiler_params=pltpu.CompilerParams(vmem_limit_bytes=4 << 20),
    )(*held)
    sum0, sum1, next0, next1, new0, new1 = outs
    return sum0, sum1, next0.T, next1.T, new0[None], new1[None]


def solution(mesh):
    wide = P("dp", None, "tensor")
    tall = P("tensor", None)
    flat = P(None, "tensor")
    return jax.shard_map(
        shards,
        mesh=mesh,
        in_specs=(wide, wide, wide, wide, tall, tall),
        out_specs=(flat, flat, tall, tall, wide, wide),
        check_vma=False,
    )
```

```python
import functools

import jax
import jax.numpy as jnp
from jax import lax
from jax.experimental import pallas as pl
from jax.experimental.pallas import tpu as pltpu
from jax.sharding import PartitionSpec as P

MESH = pl.DeviceIdType.MESH
F32, BF16 = jnp.float32, jnp.bfloat16
HIGHEST = lax.Precision.HIGHEST
NX, NY, NZ = 4, 4, 8
ROWS, RANK, WIDE = 256, 32, 1792
CH = 256
NCH = WIDE // CH
NN = (((1,), (0,)), ((), ()))
NT = (((1,), (1,)), ((), ()))
TN = (((0,), (0,)), ((), ()))


def split(value):
    high = value.astype(BF16)
    low = (value - high.astype(F32)).astype(BF16)
    return high, low


def product(a, b, dims):
    return lax.dot_general(a, b, dims, preferred_element_type=F32)


def triple(value):
    high, low = split(value)
    return jnp.concatenate([high, low, high], axis=0)


def inverse_factors(gram0, gram1):
    row = lax.broadcasted_iota(jnp.int32, (8, 128), 0)
    lane = lax.broadcasted_iota(jnp.int32, (8, 128), 1)
    first = lane < 64

    def spread(value, shape=(8, 128)):
        return jnp.broadcast_to(value, shape)

    def column(i, j):
        rows = slice(8 * i, 8 * i + 8)
        return jnp.where(first, spread(gram0[rows, j : j + 1]), spread(gram1[rows, j : j + 1]))

    parts = RANK // 8
    columns = [[column(i, j) if i >= j // 8 else None for i in range(parts)] for j in range(RANK)]
    unit = [jnp.where((lane == row + 8 * i) | (lane == row + 8 * i + 64), 1.0, 0.0) for i in range(parts)]
    pivots = [jnp.ones((8, 128), F32) for _ in range(parts)]
    for j in range(RANK):
        at, sub = j // 8, j % 8
        now = columns[j]
        pivot = spread(now[at][sub : sub + 1])
        pivots[at] = jnp.where(row == sub, pivot, pivots[at])
        if j == RANK - 1:
            break
        scale = 1.0 / pivot
        factor = [now[i] * scale if i >= at else None for i in range(parts)]
        factor[at] = jnp.where(row > sub, factor[at], 0.0)
        for k in range(j + 1, RANK):
            entry = spread(now[k // 8][k % 8 : k % 8 + 1])
            for i in range(k // 8, parts):
                columns[k][i] = columns[k][i] - factor[i] * entry
        entry = spread(unit[at][sub : sub + 1])
        for i in range(at, parts):
            unit[i] = unit[i] - factor[i] * entry
    both = jnp.concatenate([unit[i] * lax.rsqrt(pivots[i]) for i in range(parts)], axis=0)
    return both[:, :RANK], both[:, 64 : 64 + RANK]


def main_kernel(
    grad0, grad1, error0, error1, q0, q1,
    sum0, sum1, next0, next1, new0, new1,
    graw, full, qv, fhi, flo, psend, precv, cbuf, zbuf, lmine, left,
    tbuf, xr, zs, zr, tsum, wide,
    ldg, lde, ldq, s1, r1, s2, r2, s3, r3, s4, r4,
    sx, rx, sz, rz, sgz, rgz, sgx, rgx,
):
    grads, errors, qs = (grad0, grad1), (error0, error1), (q0, q1)
    sums, nexts, news = (sum0, sum1), (next0, next1), (new0, new1)
    dp, tensor = lax.axis_index("dp"), lax.axis_index("tensor")
    z, x = lax.div(dp, NX), lax.rem(dp, NX)
    y, c = lax.div(tensor, 2), lax.rem(tensor, 2)

    def device(dz=0, dx=0, dy=0, dc=0):
        return (
            lax.rem(z + dz, NZ) * NX + lax.rem(x + dx, NX),
            lax.rem(y + dy, NY) * 2 + lax.rem(c + dc, 2),
        )

    def send(src, dst, send_sem, recv_sem, to):
        pltpu.make_async_remote_copy(
            src_ref=src, dst_ref=dst, send_sem=send_sem, recv_sem=recv_sem,
            device_id=to, device_id_type=MESH,
        ).start()

    def wait(ref, sem):
        pltpu.make_async_copy(ref, ref, sem).wait()

    groups = [(0, 0, 4), (0, 4, 7), (1, 0, 4), (1, 4, 7)]

    def load(number):
        b, low, high = groups[number]
        cols = pl.ds(low * CH, (high - low) * CH)
        pltpu.make_async_copy(errors[b].at[0, :, cols], full.at[b, :, cols], lde.at[number]).start()
        pltpu.make_async_copy(grads[b].at[0, :, cols], graw.at[b, :, cols], ldg.at[number]).start()

    pltpu.make_async_copy(qs[0], qv.at[0], ldq.at[0]).start()
    for number in range(3):
        load(number)
    pltpu.make_async_copy(qs[1], qv.at[1], ldq.at[1]).start()

    barrier = pltpu.get_barrier_semaphore()
    plane = [(dx, dy) for dx in range(NX) for dy in range(NY) if (dx, dy) != (0, 0)]
    plane.sort(key=lambda d: -(min(d[0], NX - d[0]) + min(d[1], NY - d[1])))
    column = (4, 3, 5, 2, 6, 1, 7)
    peers = [device(dx=dx, dy=dy) for dx, dy in plane]
    peers += [device(dc=1)] + [device(dz=k) for k in column]
    for peer in peers:
        pl.semaphore_signal(barrier, inc=1, device_id=peer, device_id_type=MESH)

    for number, (b, low, high) in enumerate(groups):
        if low == 0:
            wait(qv.at[b], ldq.at[b])
            qhi, qlo = split(qv[b])
            both = jnp.concatenate([qhi, qlo], axis=0)
            acc = jnp.zeros((RANK, ROWS), F32)
        cols = pl.ds(low * CH, (high - low) * CH)
        wait(full.at[b, :, cols], lde.at[number])
        wait(graw.at[b, :, cols], ldg.at[number])
        if number + 3 < len(groups):
            load(number + 3)
        for j in range(low, high):
            cols = slice(j * CH, (j + 1) * CH)
            value = graw[b, :, cols].astype(F32) + full[b, :, cols]
            top, rest = split(value)
            full[b, :, cols], fhi[b, :, cols], flo[b, :, cols] = value, top, rest
            first = product(both[:, cols], top, NT)
            acc += first[:RANK] + first[RANK:] + product(qhi[:, cols], rest, NT)
        if high == NCH:
            for k in range(8):
                psend[8 * b + k] = acc[8 * (k // 2) : 8 * (k // 2) + 8, 128 * (k % 2) : 128 * (k % 2) + 128]
    pl.semaphore_wait(barrier, len(peers))

    mine = x * NY + y
    for dx, dy in plane:
        there = lax.rem(x + dx, NX) * NY + lax.rem(y + dy, NY)
        send(psend.at[there], precv.at[dx * NY + dy - 1], s1, r1, device(dx=dx, dy=dy))
    wait(precv, r1)
    part = psend[mine]
    for k in range(15):
        part += precv[k]
    cbuf[0] = part
    send(cbuf.at[0], cbuf.at[1], s2, r2, device(dc=1))
    wait(cbuf.at[1], r2)
    zbuf[0] = cbuf[0] + cbuf[1]
    for k in column:
        send(zbuf.at[0], zbuf.at[k], s3, r3, device(dz=k))
    wait(zbuf.at[pl.ds(1, 7)], r3)
    part = zbuf[z]
    for k in range(1, NZ):
        part += zbuf[lax.rem(z - k + NZ, NZ)]
    lmine[...] = part
    for dx, dy in plane:
        send(lmine, left.at[mine], s4, r4.at[lax.div(x, 2)], device(dx=dx, dy=dy))
    pltpu.make_async_copy(lmine, left.at[mine], r4.at[lax.div(x, 2)]).start()

    lefts, lhs = [], []
    for b in range(2):
        wait(left.at[pl.ds(8 * b, 8)], r4.at[b])
        rows = [jnp.concatenate([left[8 * b + 2 * k], left[8 * b + 2 * k + 1]], axis=1) for k in range(4)]
        lefts.append(jnp.concatenate(rows, axis=0))
        lhi, llo = split(lefts[b])
        lhs.append((jnp.concatenate([lhi, llo], axis=0), lhi))

    skip = NZ - 1 - z
    skip = lax.div(skip, 4) * 2 * (skip - 4) + (1 - lax.div(skip, 4)) * (7 - 2 * skip)
    order = []
    for k in range(NCH):
        i = k + lax.div(k - skip + NZ, NZ)
        order.append(lax.rem(z + 4 + (1 - 2 * lax.rem(i, 2)) * lax.div(i + 1, 2), NZ))

    def columns(chunk):
        return pl.ds(pl.multiple_of(chunk * CH, CH), CH)

    for chunk in order:
        for b in range(2):
            cols = columns(chunk)
            first = product(lhs[b][0], fhi[b, :, cols], NN)
            value = first[:RANK] + first[RANK:] + product(lhs[b][1], flo[b, :, cols], NN)
            tbuf[chunk, 2 * b] = value[:16]
            tbuf[chunk, 2 * b + 1] = value[16:]
        for dx in (2, 1, 3):
            send(
                tbuf.at[chunk, lax.rem(x + dx, NX)], xr.at[chunk, dx - 1], sx, rx.at[chunk], device(dx=dx)
            )

    for k, chunk in enumerate(order):
        wait(xr.at[chunk], rx.at[chunk])
        zs[chunk] = tbuf[chunk, x] + xr[chunk, 0] + xr[chunk, 1] + xr[chunk, 2]

        def pass_on(k=k, chunk=chunk):
            away = lax.rem(chunk - z + NZ, NZ)
            send(zs.at[chunk], zr.at[away], sz.at[k], rz, device(dz=away))

        if k < NCH - 1:
            pass_on()
        else:
            pl.when(z == NZ - 1)(pass_on)

    grams = [
        lax.dot_general(a, a, NT, precision=HIGHEST, preferred_element_type=F32) for a in lefts
    ]
    inverses = inverse_factors(*grams)
    for b in range(2):
        ortho = lax.dot_general(inverses[b], lefts[b], NN, precision=HIGHEST, preferred_element_type=F32)
        weight = lax.dot_general(inverses[b], ortho, TN, precision=HIGHEST, preferred_element_type=F32)
        weight = jnp.concatenate([weight, inverses[b].T], axis=1)
        top = weight.astype(BF16).astype(F32)
        wide[b] = jnp.concatenate([top, top, weight - top], axis=0).T.astype(BF16)

    @pl.when(z < NCH)
    def _():
        wait(zr.at[pl.ds(1, 7)], rz)
        part = zs[z]
        for k in range(1, NZ):
            part += zr[k]
        tsum[z, x] = part
        for k in column:
            send(tsum.at[z, x], tsum.at[z, x], sgz, rgz.at[z], device(dz=k))
        for dx in (2, 1, 3):
            send(tsum.at[z, x], tsum.at[z, x], sgx, rgx.at[z, dx - 1], device(dx=dx))

    for b in range(2):
        for j in range(NCH):
            own = tbuf[j, 2 * b : 2 * b + 2].reshape(RANK, CH)
            cols = slice(j * CH, (j + 1) * CH)
            news[b][:, cols] = full[b, :, cols] - product(wide[b, :ROWS], triple(own), NN)

    for k in reversed(range(NCH)):

        def forward(chunk=order[k]):
            wait(tsum.at[chunk, x], rgz.at[chunk])
            for dx in (2, 1, 3):
                send(tsum.at[chunk, x], tsum.at[chunk, x], sgx, rgx.at[chunk, dx - 1], device(dx=dx))

        if k < NCH - 1:
            forward()
        else:
            pl.when(z == NZ - 1)(forward)

    for chunk in reversed(order):
        for dx in (1, 3, 2):
            wait(tsum.at[chunk, lax.rem(x - dx + NX, NX)], rgx.at[chunk, dx - 1])
        cols = columns(chunk)
        for b in range(2):
            total = tsum[chunk, 2 * b : 2 * b + 2].reshape(RANK, CH)
            value = product(wide[b], triple(total), NN)
            sums[b][:, cols] = value[:ROWS].astype(BF16)
            nexts[b][:, cols] = value[ROWS:]

    wait(precv, s1)
    wait(cbuf.at[1], s2)
    wait(zbuf.at[pl.ds(1, 7)], s3)
    wait(precv, s4)
    wait(xr, sx)
    wait(xr, sgx)
    for k in range(NCH - 1):
        wait(zs.at[k], sz.at[k])

    @pl.when(z == NZ - 1)
    def _():
        wait(zs.at[0], sz.at[NCH - 1])

    @pl.when(z < NCH)
    def _():
        wait(zr.at[pl.ds(1, 7)], sgz)


def store_kernel(*refs):
    ins, outs, sem = refs[:6], refs[6:12], refs[12]
    copies = [pltpu.make_async_copy(a, b, sem.at[i]) for i, (a, b) in enumerate(zip(ins, outs))]
    for copy in copies:
        copy.start()
    for copy in copies:
        copy.wait()


def shards(grad0, grad1, error0, error1, q0, q1):
    args = (grad0, grad1, error0, error1, q0.T, q1.T)
    vmem = pl.BlockSpec(memory_space=pltpu.VMEM)
    hbm = pl.BlockSpec(memory_space=pltpu.HBM)
    shapes = [
        ((ROWS, WIDE), BF16), ((ROWS, WIDE), BF16),
        ((RANK, WIDE), F32), ((RANK, WIDE), F32),
        ((ROWS, WIDE), F32), ((ROWS, WIDE), F32),
    ]
    dma = pltpu.SemaphoreType.DMA
    scratch = [
        pltpu.VMEM((2, ROWS, WIDE), BF16),
        pltpu.VMEM((2, ROWS, WIDE), F32),
        pltpu.VMEM((2, RANK, WIDE), F32),
        pltpu.VMEM((2, ROWS, WIDE), BF16),
        pltpu.VMEM((2, ROWS, WIDE), BF16),
        pltpu.VMEM((16, 8, 128), F32),
        pltpu.VMEM((15, 8, 128), F32),
        pltpu.VMEM((2, 8, 128), F32),
        pltpu.VMEM((NZ, 8, 128), F32),
        pltpu.VMEM((8, 128), F32),
        pltpu.VMEM((16, 8, 128), F32),
        pltpu.VMEM((NCH, NX, 16, CH), F32),
        pltpu.VMEM((NCH, NX - 1, 16, CH), F32),
        pltpu.VMEM((NCH, 16, CH), F32),
        pltpu.VMEM((NZ, 16, CH), F32),
        pltpu.VMEM((NCH, NX, 16, CH), F32),
        pltpu.VMEM((2, ROWS + RANK, 3 * RANK), BF16),
        dma((4,)), dma((4,)), dma((2,)),
        dma, dma, dma, dma, dma, dma, dma, dma((2,)),
        dma, dma((NCH,)), dma((NCH,)), dma,
        dma, dma((NCH,)), dma, dma((NCH, NX - 1)),
    ]
    held = pl.pallas_call(
        main_kernel,
        out_shape=[pltpu.VMEM(s, d) for s, d in shapes],
        in_specs=[hbm] * 6,
        out_specs=[vmem] * 6,
        scratch_shapes=scratch,
        name="compress",
        compiler_params=pltpu.CompilerParams(
            collective_id=0, has_side_effects=True, vmem_limit_bytes=36 << 20
        ),
    )(*[pltpu.with_memory_space_constraint(a, pltpu.HBM) for a in args])
    outs = pl.pallas_call(
        store_kernel,
        out_shape=[jax.ShapeDtypeStruct(s, d) for s, d in shapes],
        in_specs=[vmem] * 6,
        out_specs=[hbm] * 6,
        scratch_shapes=[dma((6,))],
        name="store",
        compiler_params=pltpu.CompilerParams(vmem_limit_bytes=4 << 20),
    )(*held)
    sum0, sum1, next0, next1, new0, new1 = outs
    return sum0, sum1, next0.T, next1.T, new0[None], new1[None]


def solution(mesh):
    wide = P("dp", None, "tensor")
    tall = P("tensor", None)
    flat = P(None, "tensor")
    return jax.shard_map(
        shards,
        mesh=mesh,
        in_specs=(wide, wide, wide, wide, tall, tall),
        out_specs=(flat, flat, tall, tall, wide, wide),
        check_vma=False,
    )
```

```python
import functools

import jax
import jax.numpy as jnp
from jax import lax
from jax.experimental import pallas as pl
from jax.experimental.pallas import tpu as pltpu
from jax.sharding import PartitionSpec as P

MESH = pl.DeviceIdType.MESH
F32, BF16 = jnp.float32, jnp.bfloat16
HIGHEST = lax.Precision.HIGHEST
NX, NY, NZ = 4, 4, 8
ROWS, RANK, WIDE = 256, 32, 1792
CH = 256
NCH = WIDE // CH
BARE = 4
NN = (((1,), (0,)), ((), ()))
NT = (((1,), (1,)), ((), ()))
TN = (((0,), (0,)), ((), ()))


def split(value):
    high = value.astype(BF16)
    low = (value - high.astype(F32)).astype(BF16)
    return high, low


def product(a, b, dims):
    return lax.dot_general(a, b, dims, preferred_element_type=F32)


def triple(value):
    high, low = split(value)
    return jnp.concatenate([high, low, high], axis=0)


def inverse_factors(gram0, gram1):
    row = lax.broadcasted_iota(jnp.int32, (8, 128), 0)
    lane = lax.broadcasted_iota(jnp.int32, (8, 128), 1)
    first = lane < 64

    def spread(value, shape=(8, 128)):
        return jnp.broadcast_to(value, shape)

    def column(i, j):
        rows = slice(8 * i, 8 * i + 8)
        return jnp.where(first, spread(gram0[rows, j : j + 1]), spread(gram1[rows, j : j + 1]))

    parts = RANK // 8
    columns = [[column(i, j) if i >= j // 8 else None for i in range(parts)] for j in range(RANK)]
    unit = [jnp.where((lane == row + 8 * i) | (lane == row + 8 * i + 64), 1.0, 0.0) for i in range(parts)]
    pivots = [jnp.ones((8, 128), F32) for _ in range(parts)]
    for j in range(RANK):
        at, sub = j // 8, j % 8
        now = columns[j]
        pivot = spread(now[at][sub : sub + 1])
        pivots[at] = jnp.where(row == sub, pivot, pivots[at])
        if j == RANK - 1:
            break
        scale = 1.0 / pivot
        factor = [now[i] * scale if i >= at else None for i in range(parts)]
        factor[at] = jnp.where(row > sub, factor[at], 0.0)
        for k in range(j + 1, RANK):
            entry = spread(now[k // 8][k % 8 : k % 8 + 1])
            for i in range(k // 8, parts):
                columns[k][i] = columns[k][i] - factor[i] * entry
        entry = spread(unit[at][sub : sub + 1])
        for i in range(at, parts):
            unit[i] = unit[i] - factor[i] * entry
    both = jnp.concatenate([unit[i] * lax.rsqrt(pivots[i]) for i in range(parts)], axis=0)
    return both[:, :RANK], both[:, 64 : 64 + RANK]


def main_kernel(
    grad0, grad1, error0, error1, q0, q1,
    tsum, wide, new0, new1,
    graw, full, qv, fhi, flo, psend, precv, cbuf, zbuf, lmine, left,
    tbuf, xr, zs, zr,
    ldg, lde, ldq, s1, r1, s2, r2, s3, r3, s4, r4,
    sx, rx, sz, rz, sgz, rgz, sgx, rgx,
):
    grads, errors, qs = (grad0, grad1), (error0, error1), (q0, q1)
    news = (new0, new1)
    dp, tensor = lax.axis_index("dp"), lax.axis_index("tensor")
    z, x = lax.div(dp, NX), lax.rem(dp, NX)
    y, c = lax.div(tensor, 2), lax.rem(tensor, 2)

    def device(dz=0, dx=0, dy=0, dc=0):
        return (
            lax.rem(z + dz, NZ) * NX + lax.rem(x + dx, NX),
            lax.rem(y + dy, NY) * 2 + lax.rem(c + dc, 2),
        )

    def send(src, dst, send_sem, recv_sem, to):
        pltpu.make_async_remote_copy(
            src_ref=src, dst_ref=dst, send_sem=send_sem, recv_sem=recv_sem,
            device_id=to, device_id_type=MESH,
        ).start()

    def wait(ref, sem):
        pltpu.make_async_copy(ref, ref, sem).wait()

    groups = [(0, 0, 4), (0, 4, 7), (1, 0, 4), (1, 4, 7)]

    def load(number):
        b, low, high = groups[number]
        cols = pl.ds(low * CH, (high - low) * CH)
        pltpu.make_async_copy(errors[b].at[0, :, cols], full.at[b, :, cols], lde.at[number]).start()
        pltpu.make_async_copy(grads[b].at[0, :, cols], graw.at[b, :, cols], ldg.at[number]).start()

    pltpu.make_async_copy(qs[0], qv.at[0], ldq.at[0]).start()
    for number in range(3):
        load(number)
    pltpu.make_async_copy(qs[1], qv.at[1], ldq.at[1]).start()

    barrier = pltpu.get_barrier_semaphore()
    plane = [(dx, dy) for dx in range(NX) for dy in range(NY) if (dx, dy) != (0, 0)]
    plane.sort(key=lambda d: -(min(d[0], NX - d[0]) + min(d[1], NY - d[1])))
    column = (4, 3, 5, 2, 6, 1, 7)
    peers = [device(dx=dx, dy=dy) for dx, dy in plane]
    peers += [device(dc=1)] + [device(dz=k) for k in column]
    for peer in peers:
        pl.semaphore_signal(barrier, inc=1, device_id=peer, device_id_type=MESH)

    for number, (b, low, high) in enumerate(groups):
        if low == 0:
            wait(qv.at[b], ldq.at[b])
            qhi, qlo = split(qv[b])
            both = jnp.concatenate([qhi, qlo], axis=0)
            acc = jnp.zeros((RANK, ROWS), F32)
        cols = pl.ds(low * CH, (high - low) * CH)
        wait(full.at[b, :, cols], lde.at[number])
        wait(graw.at[b, :, cols], ldg.at[number])
        if number + 3 < len(groups):
            load(number + 3)
        for j in range(low, high):
            cols = slice(j * CH, (j + 1) * CH)
            value = graw[b, :, cols].astype(F32) + full[b, :, cols]
            top, rest = split(value)
            full[b, :, cols], fhi[b, :, cols], flo[b, :, cols] = value, top, rest
            first = product(both[:, cols], top, NT)
            acc += first[:RANK] + first[RANK:] + product(qhi[:, cols], rest, NT)
        if high < NCH:
            continue
        for k in range(8):
            psend[8 * b + k] = acc[8 * (k // 2) : 8 * (k // 2) + 8, 128 * (k % 2) : 128 * (k % 2) + 128]
        if b == 0:
            pl.semaphore_wait(barrier, len(peers))
        for xo in (2 * b, 2 * b + 1):
            for dy in (2, 1, 3, 0):

                def give(xo=xo, dy=dy):
                    yo = lax.rem(y + dy, NY)
                    slot = lax.rem(xo - x + NX, NX) * NY + dy - 1
                    to = (z * NX + xo, yo * 2 + c)
                    send(psend.at[xo * NY + yo], precv.at[slot], s1, r1, to)

                if dy:
                    give()
                else:
                    pl.when(x != xo)(give)

    mine = x * NY + y
    wait(precv, r1)
    part = psend[mine]
    for k in range(15):
        part += precv[k]
    cbuf[0] = part
    send(cbuf.at[0], cbuf.at[1], s2, r2, device(dc=1))
    wait(cbuf.at[1], r2)
    zbuf[0] = cbuf[0] + cbuf[1]
    for k in column:
        send(zbuf.at[0], zbuf.at[k], s3, r3, device(dz=k))
    wait(zbuf.at[pl.ds(1, 7)], r3)
    part = zbuf[z]
    for k in range(1, NZ):
        part += zbuf[lax.rem(z - k + NZ, NZ)]
    lmine[...] = part
    for dx, dy in plane:
        send(lmine, left.at[mine], s4, r4.at[lax.div(x, 2)], device(dx=dx, dy=dy))
    pltpu.make_async_copy(lmine, left.at[mine], r4.at[lax.div(x, 2)]).start()

    skip = lax.rem(BARE - z + NZ, NZ)
    skip = lax.div(skip, 4) * 2 * (skip - 4) + (1 - lax.div(skip, 4)) * (7 - 2 * skip)
    order = []
    for k in range(NCH):
        i = k + lax.div(k - skip + NZ, NZ)
        away = lax.rem(4 + (1 - 2 * lax.rem(i, 2)) * lax.div(i + 1, 2), NZ)
        order.append((lax.rem(z + away + NZ - 1 - BARE, NZ), away))
    owned = lax.rem(z + NZ - 1 - BARE, NZ)

    lefts = []
    for b in range(2):
        wait(left.at[pl.ds(8 * b, 8)], r4.at[b])
        rows = [jnp.concatenate([left[8 * b + 2 * k], left[8 * b + 2 * k + 1]], axis=1) for k in range(4)]
        lefts.append(jnp.concatenate(rows, axis=0))
        lhi, llo = split(lefts[b])
        both = jnp.concatenate([lhi, llo], axis=0)
        for chunk, _ in order:
            cols = pl.ds(pl.multiple_of(chunk * CH, CH), CH)
            first = product(both, fhi[b, :, cols], NN)
            value = first[:RANK] + first[RANK:] + product(lhi, flo[b, :, cols], NN)
            tbuf[chunk, b] = value.reshape(NX, 8, CH)
            for dx in (2, 1, 3):
                src = tbuf.at[chunk, b, lax.rem(x + dx, NX)]
                send(src, xr.at[chunk, b, dx - 1], sx, rx.at[b, chunk], device(dx=dx))

    for b in range(2):
        for k, (chunk, away) in enumerate(order):
            wait(xr.at[chunk, b], rx.at[b, chunk])
            zs[b, chunk] = tbuf[chunk, b, x] + xr[chunk, b, 0] + xr[chunk, b, 1] + xr[chunk, b, 2]

            def pass_on(b=b, k=k, chunk=chunk, away=away):
                send(zs.at[b, chunk], zr.at[b, away], sz.at[b, k], rz.at[b], device(dz=away))

            if k < NCH - 1:
                pass_on()
            else:
                pl.when(z == BARE)(pass_on)

    grams = [
        lax.dot_general(a, a, NT, precision=HIGHEST, preferred_element_type=F32) for a in lefts
    ]
    inverses = inverse_factors(*grams)
    for b in range(2):
        ortho = lax.dot_general(inverses[b], lefts[b], NN, precision=HIGHEST, preferred_element_type=F32)
        weight = lax.dot_general(inverses[b], ortho, TN, precision=HIGHEST, preferred_element_type=F32)
        weight = jnp.concatenate([weight, inverses[b].T], axis=1)
        top = weight.astype(BF16).astype(F32)
        wide[b] = jnp.concatenate([top, top, weight - top], axis=0).T.astype(BF16)

    for b in range(2):

        @pl.when(z != BARE)
        def _():
            wait(zr.at[b, pl.ds(1, 7)], rz.at[b])
            part = zs[b, owned]
            for k in range(1, NZ):
                part += zr[b, k]
            tsum[owned, b, x] = part
            here = tsum.at[owned, b, x]
            for k in column:
                send(here, here, sgz.at[b], rgz.at[b, owned], device(dz=k))
            for dx in (2, 1, 3):
                send(here, here, sgx, rgx, device(dx=dx))

    for b in range(2):
        for j in range(NCH):
            own = tbuf[j, b].reshape(RANK, CH)
            cols = slice(j * CH, (j + 1) * CH)
            news[b][:, cols] = full[b, :, cols] - product(wide[b, :ROWS], triple(own), NN)

    for b in range(2):
        for k in reversed(range(NCH)):

            def forward(b=b, chunk=order[k][0]):
                here = tsum.at[chunk, b, x]
                wait(here, rgz.at[b, chunk])
                for dx in (2, 1, 3):
                    send(here, here, sgx, rgx, device(dx=dx))

            if k < NCH - 1:
                forward()
            else:
                pl.when(z == BARE)(forward)

    wait(xr, rgx)

    wait(precv, s1)
    wait(cbuf.at[1], s2)
    wait(zbuf.at[pl.ds(1, 7)], s3)
    wait(precv, s4)
    wait(xr, sx)
    wait(xr, sgx)
    for b in range(2):
        for k in range(NCH - 1):
            wait(zs.at[b, k], sz.at[b, k])

        @pl.when(z == BARE)
        def _():
            wait(zs.at[b, 0], sz.at[b, NCH - 1])

        @pl.when(z != BARE)
        def _():
            wait(zr.at[b, pl.ds(1, 7)], sgz.at[b])


def finish_kernel(
    tsum, wide, new0, new1, sum0, sum1, next0, next1, out0, out1, sums, nexts, sem
):
    copies = [pltpu.make_async_copy(new0, out0, sem.at[0]), pltpu.make_async_copy(new1, out1, sem.at[1])]
    for copy in copies:
        copy.start()
    for low, high in ((0, 4), (4, 7)):
        for b in range(2):
            for j in range(low, high):
                cols = slice(j * CH, (j + 1) * CH)
                value = product(wide[b], triple(tsum[j, b].reshape(RANK, CH)), NN)
                sums[b, :, cols] = value[:ROWS].astype(BF16)
                nexts[b, :, cols] = value[ROWS:]
            cols = pl.ds(low * CH, (high - low) * CH)
            for held, out in ((sums, (sum0, sum1)), (nexts, (next0, next1))):
                copy = pltpu.make_async_copy(held.at[b, :, cols], out[b].at[:, cols], sem.at[len(copies)])
                copy.start()
                copies.append(copy)
    for copy in copies:
        copy.wait()


def shards(grad0, grad1, error0, error1, q0, q1):
    args = (grad0, grad1, error0, error1, q0.T, q1.T)
    vmem = pl.BlockSpec(memory_space=pltpu.VMEM)
    hbm = pl.BlockSpec(memory_space=pltpu.HBM)
    dma = pltpu.SemaphoreType.DMA
    scratch = [
        pltpu.VMEM((2, ROWS, WIDE), BF16),
        pltpu.VMEM((2, ROWS, WIDE), F32),
        pltpu.VMEM((2, RANK, WIDE), F32),
        pltpu.VMEM((2, ROWS, WIDE), BF16),
        pltpu.VMEM((2, ROWS, WIDE), BF16),
        pltpu.VMEM((16, 8, 128), F32),
        pltpu.VMEM((15, 8, 128), F32),
        pltpu.VMEM((2, 8, 128), F32),
        pltpu.VMEM((NZ, 8, 128), F32),
        pltpu.VMEM((8, 128), F32),
        pltpu.VMEM((16, 8, 128), F32),
        pltpu.VMEM((NCH, 2, NX, 8, CH), F32),
        pltpu.VMEM((NCH, 2, NX - 1, 8, CH), F32),
        pltpu.VMEM((2, NCH, 8, CH), F32),
        pltpu.VMEM((2, NZ, 8, CH), F32),
        dma((4,)), dma((4,)), dma((2,)),
        dma, dma, dma, dma, dma, dma, dma, dma((2,)),
        dma, dma((2, NCH)), dma((2, NCH)), dma((2,)),
        dma((2,)), dma((2, NCH)), dma, dma,
    ]
    held = pl.pallas_call(
        main_kernel,
        out_shape=[
            pltpu.VMEM((NCH, 2, NX, 8, CH), F32),
            pltpu.VMEM((2, ROWS + RANK, 3 * RANK), BF16),
            pltpu.VMEM((ROWS, WIDE), F32),
            pltpu.VMEM((ROWS, WIDE), F32),
        ],
        in_specs=[hbm] * 6,
        out_specs=[vmem] * 4,
        scratch_shapes=scratch,
        name="compress",
        compiler_params=pltpu.CompilerParams(
            collective_id=0, has_side_effects=True, vmem_limit_bytes=36 << 20
        ),
    )(*[pltpu.with_memory_space_constraint(a, pltpu.HBM) for a in args])
    sum0, sum1, next0, next1, new0, new1 = pl.pallas_call(
        finish_kernel,
        out_shape=[
            jax.ShapeDtypeStruct((ROWS, WIDE), BF16),
            jax.ShapeDtypeStruct((ROWS, WIDE), BF16),
            jax.ShapeDtypeStruct((RANK, WIDE), F32),
            jax.ShapeDtypeStruct((RANK, WIDE), F32),
            jax.ShapeDtypeStruct((ROWS, WIDE), F32),
            jax.ShapeDtypeStruct((ROWS, WIDE), F32),
        ],
        in_specs=[vmem] * 4,
        out_specs=[hbm] * 6,
        scratch_shapes=[
            pltpu.VMEM((2, ROWS, WIDE), BF16),
            pltpu.VMEM((2, RANK, WIDE), F32),
            dma((10,)),
        ],
        name="finish",
        compiler_params=pltpu.CompilerParams(vmem_limit_bytes=8 << 20),
    )(*held)
    return sum0, sum1, next0.T, next1.T, new0[None], new1[None]


def solution(mesh):
    wide = P("dp", None, "tensor")
    tall = P("tensor", None)
    flat = P(None, "tensor")
    return jax.shard_map(
        shards,
        mesh=mesh,
        in_specs=(wide, wide, wide, wide, tall, tall),
        out_specs=(flat, flat, tall, tall, wide, wide),
        check_vma=False,
    )
```

```python
import functools

import jax
import jax.numpy as jnp
from jax import lax
from jax.experimental import pallas as pl
from jax.experimental.pallas import tpu as pltpu
from jax.sharding import PartitionSpec as P

MESH = pl.DeviceIdType.MESH
F32, BF16 = jnp.float32, jnp.bfloat16
HIGHEST = lax.Precision.HIGHEST
NX, NY, NZ = 4, 4, 8
ROWS, RANK, WIDE = 256, 32, 1792
CH = 256
NCH = WIDE // CH
BARE = 4
NN = (((1,), (0,)), ((), ()))
NT = (((1,), (1,)), ((), ()))
TN = (((0,), (0,)), ((), ()))


def split(value):
    high = value.astype(BF16)
    low = (value - high.astype(F32)).astype(BF16)
    return high, low


def product(a, b, dims):
    return lax.dot_general(a, b, dims, preferred_element_type=F32)


def triple(value):
    high, low = split(value)
    return jnp.concatenate([high, low, high], axis=0)


def inverse_factors(gram0, gram1):
    row = lax.broadcasted_iota(jnp.int32, (8, 128), 0)
    lane = lax.broadcasted_iota(jnp.int32, (8, 128), 1)
    first = lane < 64

    def spread(value, shape=(8, 128)):
        return jnp.broadcast_to(value, shape)

    def column(i, j):
        rows = slice(8 * i, 8 * i + 8)
        return jnp.where(first, spread(gram0[rows, j : j + 1]), spread(gram1[rows, j : j + 1]))

    parts = RANK // 8
    columns = [[column(i, j) if i >= j // 8 else None for i in range(parts)] for j in range(RANK)]
    unit = [jnp.where((lane == row + 8 * i) | (lane == row + 8 * i + 64), 1.0, 0.0) for i in range(parts)]
    pivots = [jnp.ones((8, 128), F32) for _ in range(parts)]
    for j in range(RANK):
        at, sub = j // 8, j % 8
        now = columns[j]
        pivot = spread(now[at][sub : sub + 1])
        pivots[at] = jnp.where(row == sub, pivot, pivots[at])
        if j == RANK - 1:
            break
        scale = 1.0 / pivot
        factor = [now[i] * scale if i >= at else None for i in range(parts)]
        factor[at] = jnp.where(row > sub, factor[at], 0.0)
        for k in range(j + 1, RANK):
            entry = spread(now[k // 8][k % 8 : k % 8 + 1])
            for i in range(k // 8, parts):
                columns[k][i] = columns[k][i] - factor[i] * entry
        entry = spread(unit[at][sub : sub + 1])
        for i in range(at, parts):
            unit[i] = unit[i] - factor[i] * entry
    both = jnp.concatenate([unit[i] * lax.rsqrt(pivots[i]) for i in range(parts)], axis=0)
    return both[:, :RANK], both[:, 64 : 64 + RANK]


def main_kernel(
    grad0, grad1, error0, error1, q0, q1,
    tsum, wide, new0, new1,
    graw, full, qv, fhi, flo, psend, precv, zbuf, lmine, left,
    tbuf, xr, zs, zr,
    ldg, lde, ldq, s1, r1, s3, r3, s4, r4,
    sx, rx, sz, rz, sgz, rgz, sgx, rgx,
):
    grads, errors, qs = (grad0, grad1), (error0, error1), (q0, q1)
    news = (new0, new1)
    dp, tensor = lax.axis_index("dp"), lax.axis_index("tensor")
    z, x = lax.div(dp, NX), lax.rem(dp, NX)
    y, c = lax.div(tensor, 2), lax.rem(tensor, 2)

    def device(dz=0, dx=0, dy=0, dc=0):
        return (
            lax.rem(z + dz, NZ) * NX + lax.rem(x + dx, NX),
            lax.rem(y + dy, NY) * 2 + lax.rem(c + dc, 2),
        )

    def send(src, dst, send_sem, recv_sem, to):
        pltpu.make_async_remote_copy(
            src_ref=src, dst_ref=dst, send_sem=send_sem, recv_sem=recv_sem,
            device_id=to, device_id_type=MESH,
        ).start()

    def wait(ref, sem):
        pltpu.make_async_copy(ref, ref, sem).wait()

    groups = [(0, 0, 4), (0, 4, 7), (1, 0, 4), (1, 4, 7)]

    def load(number):
        b, low, high = groups[number]
        cols = pl.ds(low * CH, (high - low) * CH)
        pltpu.make_async_copy(errors[b].at[0, :, cols], full.at[b, :, cols], lde.at[number]).start()
        pltpu.make_async_copy(grads[b].at[0, :, cols], graw.at[b, :, cols], ldg.at[number]).start()

    pltpu.make_async_copy(qs[0], qv.at[0], ldq.at[0]).start()
    for number in range(3):
        load(number)
    pltpu.make_async_copy(qs[1], qv.at[1], ldq.at[1]).start()

    barrier = pltpu.get_barrier_semaphore()
    plane = [(dx, dy) for dx in range(NX) for dy in range(NY) if (dx, dy) != (0, 0)]
    plane.sort(key=lambda d: -(min(d[0], NX - d[0]) + min(d[1], NY - d[1])))
    column = (4, 3, 5, 2, 6, 1, 7)
    peers = [device(dx=dx, dy=dy) for dx, dy in plane]
    peers += [device(dc=1)] + [device(dz=k, dc=dc) for k in column for dc in range(2)]
    for peer in peers:
        pl.semaphore_signal(barrier, inc=1, device_id=peer, device_id_type=MESH)

    for number, (b, low, high) in enumerate(groups):
        if low == 0:
            wait(qv.at[b], ldq.at[b])
            qhi, qlo = split(qv[b])
            both = jnp.concatenate([qhi, qlo], axis=0)
            acc = jnp.zeros((RANK, ROWS), F32)
        cols = pl.ds(low * CH, (high - low) * CH)
        wait(full.at[b, :, cols], lde.at[number])
        wait(graw.at[b, :, cols], ldg.at[number])
        if number + 3 < len(groups):
            load(number + 3)
        for j in range(low, high):
            cols = slice(j * CH, (j + 1) * CH)
            value = graw[b, :, cols].astype(F32) + full[b, :, cols]
            top, rest = split(value)
            full[b, :, cols], fhi[b, :, cols], flo[b, :, cols] = value, top, rest
            first = product(both[:, cols], top, NT)
            acc += first[:RANK] + first[RANK:] + product(qhi[:, cols], rest, NT)
        if high < NCH:
            continue
        for k in range(8):
            psend[8 * b + k] = acc[8 * (k // 2) : 8 * (k // 2) + 8, 128 * (k % 2) : 128 * (k % 2) + 128]
        if b == 0:
            pl.semaphore_wait(barrier, len(peers))
        for xo in (2 * b, 2 * b + 1):
            for dy in (2, 1, 3, 0):

                def give(xo=xo, dy=dy):
                    yo = lax.rem(y + dy, NY)
                    slot = lax.rem(xo - x + NX, NX) * NY + dy - 1
                    to = (z * NX + xo, yo * 2 + c)
                    send(psend.at[xo * NY + yo], precv.at[slot], s1, r1, to)

                if dy:
                    give()
                else:
                    pl.when(x != xo)(give)

    mine = x * NY + y
    wait(precv, r1)
    part = psend[mine]
    for k in range(15):
        part += precv[k]
    zbuf[0] = part
    for k in column:
        for dc in (1, 0):
            send(zbuf.at[0], zbuf.at[2 * k + dc], s3, r3, device(dz=k, dc=dc))
    send(zbuf.at[0], zbuf.at[1], s3, r3, device(dc=1))
    wait(zbuf.at[pl.ds(1, 15)], r3)
    part = zbuf[2 * z + c]
    for k in range(1, 2 * NZ):
        part += zbuf[2 * lax.rem(z - k // 2 + NZ, NZ) + lax.rem(c + k, 2)]
    lmine[...] = part
    for dx, dy in plane:
        send(lmine, left.at[mine], s4, r4.at[lax.div(x, 2)], device(dx=dx, dy=dy))
    pltpu.make_async_copy(lmine, left.at[mine], r4.at[lax.div(x, 2)]).start()

    skip = lax.rem(BARE - z + NZ, NZ)
    skip = lax.div(skip, 4) * 2 * (skip - 4) + (1 - lax.div(skip, 4)) * (7 - 2 * skip)
    order = []
    for k in range(NCH):
        i = k + lax.div(k - skip + NZ, NZ)
        away = lax.rem(4 + (1 - 2 * lax.rem(i, 2)) * lax.div(i + 1, 2), NZ)
        order.append((lax.rem(z + away + NZ - 1 - BARE, NZ), away))
    owned = lax.rem(z + NZ - 1 - BARE, NZ)

    lefts = []
    for b in range(2):
        wait(left.at[pl.ds(8 * b, 8)], r4.at[b])
        rows = [jnp.concatenate([left[8 * b + 2 * k], left[8 * b + 2 * k + 1]], axis=1) for k in range(4)]
        lefts.append(jnp.concatenate(rows, axis=0))
        lhi, llo = split(lefts[b])
        both = jnp.concatenate([lhi, llo], axis=0)
        for chunk, _ in order:
            cols = pl.ds(pl.multiple_of(chunk * CH, CH), CH)
            first = product(both, fhi[b, :, cols], NN)
            value = first[:RANK] + first[RANK:] + product(lhi, flo[b, :, cols], NN)
            tbuf[chunk, b] = value.reshape(NX, 8, CH)
            for dx in (2, 1, 3):
                src = tbuf.at[chunk, b, lax.rem(x + dx, NX)]
                send(src, xr.at[chunk, b, dx - 1], sx, rx.at[b, chunk], device(dx=dx))

    for b in range(2):
        for k, (chunk, away) in enumerate(order):
            wait(xr.at[chunk, b], rx.at[b, chunk])
            zs[b, chunk] = tbuf[chunk, b, x] + xr[chunk, b, 0] + xr[chunk, b, 1] + xr[chunk, b, 2]

            def pass_on(b=b, k=k, chunk=chunk, away=away):
                send(zs.at[b, chunk], zr.at[b, away], sz.at[b, k // 6], rz.at[b], device(dz=away))

            if k < NCH - 1:
                pass_on()
            else:
                pl.when(z == BARE)(pass_on)

    grams = [
        lax.dot_general(a, a, NT, precision=HIGHEST, preferred_element_type=F32) for a in lefts
    ]
    inverses = inverse_factors(*grams)
    for b in range(2):
        ortho = lax.dot_general(inverses[b], lefts[b], NN, precision=HIGHEST, preferred_element_type=F32)
        weight = lax.dot_general(inverses[b], ortho, TN, precision=HIGHEST, preferred_element_type=F32)
        weight = jnp.concatenate([weight, inverses[b].T], axis=1)
        top = weight.astype(BF16).astype(F32)
        wide[b] = jnp.concatenate([top, top, weight - top], axis=0).T.astype(BF16)

    for b in range(2):

        @pl.when(z != BARE)
        def _():
            wait(zr.at[b, pl.ds(1, 7)], rz.at[b])
            part = zs[b, owned]
            for k in range(1, NZ):
                part += zr[b, k]
            tsum[owned, b, x] = part
            here = tsum.at[owned, b, x]
            for k in column:
                send(here, here, sgz.at[b], rgz.at[b, owned], device(dz=k))
            for dx in (2, 1, 3):
                send(here, here, sgx, rgx, device(dx=dx))

    for b in range(2):
        for j in range(NCH):
            own = tbuf[j, b].reshape(RANK, CH)
            cols = slice(j * CH, (j + 1) * CH)
            news[b][:, cols] = full[b, :, cols] - product(wide[b, :ROWS], triple(own), NN)

    wait(precv, s1)
    wait(zbuf.at[pl.ds(1, 15)], s3)
    wait(precv, s4)
    wait(xr, sx)
    for b in range(2):
        wait(zs.at[b, pl.ds(0, 6)], sz.at[b, 0])

        @pl.when(z == BARE)
        def _():
            wait(zs.at[b, 0], sz.at[b, 1])

        @pl.when(z != BARE)
        def _():
            wait(zr.at[b, pl.ds(1, 7)], sgz.at[b])

    for b in range(2):
        for k in reversed(range(NCH)):

            def forward(b=b, chunk=order[k][0]):
                here = tsum.at[chunk, b, x]
                wait(here, rgz.at[b, chunk])
                for dx in (2, 1, 3):
                    send(here, here, sgx, rgx, device(dx=dx))

            if k < NCH - 1:
                forward()
            else:
                pl.when(z == BARE)(forward)

    wait(xr, rgx)

    wait(xr, sgx)


def finish_kernel(
    tsum, wide, new0, new1, sum0, sum1, next0, next1, out0, out1, sums, nexts, sem
):
    copies = [pltpu.make_async_copy(new0, out0, sem.at[0]), pltpu.make_async_copy(new1, out1, sem.at[1])]
    for copy in copies:
        copy.start()
    for low, high in ((0, 4), (4, 7)):
        for b in range(2):
            for j in range(low, high):
                cols = slice(j * CH, (j + 1) * CH)
                value = product(wide[b], triple(tsum[j, b].reshape(RANK, CH)), NN)
                sums[b, :, cols] = value[:ROWS].astype(BF16)
                nexts[b, :, cols] = value[ROWS:]
            cols = pl.ds(low * CH, (high - low) * CH)
            for held, out in ((sums, (sum0, sum1)), (nexts, (next0, next1))):
                copy = pltpu.make_async_copy(held.at[b, :, cols], out[b].at[:, cols], sem.at[len(copies)])
                copy.start()
                copies.append(copy)
    for copy in copies:
        copy.wait()


def shards(grad0, grad1, error0, error1, q0, q1):
    args = (grad0, grad1, error0, error1, q0.T, q1.T)
    vmem = pl.BlockSpec(memory_space=pltpu.VMEM)
    hbm = pl.BlockSpec(memory_space=pltpu.HBM)
    dma = pltpu.SemaphoreType.DMA
    scratch = [
        pltpu.VMEM((2, ROWS, WIDE), BF16),
        pltpu.VMEM((2, ROWS, WIDE), F32),
        pltpu.VMEM((2, RANK, WIDE), F32),
        pltpu.VMEM((2, ROWS, WIDE), BF16),
        pltpu.VMEM((2, ROWS, WIDE), BF16),
        pltpu.VMEM((16, 8, 128), F32),
        pltpu.VMEM((15, 8, 128), F32),
        pltpu.VMEM((2 * NZ, 8, 128), F32),
        pltpu.VMEM((8, 128), F32),
        pltpu.VMEM((16, 8, 128), F32),
        pltpu.VMEM((NCH, 2, NX, 8, CH), F32),
        pltpu.VMEM((NCH, 2, NX - 1, 8, CH), F32),
        pltpu.VMEM((2, NCH, 8, CH), F32),
        pltpu.VMEM((2, NZ, 8, CH), F32),
        dma((4,)), dma((4,)), dma((2,)),
        dma, dma, dma, dma, dma, dma((2,)),
        dma, dma((2, NCH)), dma((2, 2)), dma((2,)),
        dma((2,)), dma((2, NCH)), dma, dma,
    ]
    held = pl.pallas_call(
        main_kernel,
        out_shape=[
            pltpu.VMEM((NCH, 2, NX, 8, CH), F32),
            pltpu.VMEM((2, ROWS + RANK, 3 * RANK), BF16),
            pltpu.VMEM((ROWS, WIDE), F32),
            pltpu.VMEM((ROWS, WIDE), F32),
        ],
        in_specs=[hbm] * 6,
        out_specs=[vmem] * 4,
        scratch_shapes=scratch,
        name="compress",
        compiler_params=pltpu.CompilerParams(
            collective_id=0, has_side_effects=True, vmem_limit_bytes=36 << 20
        ),
    )(*[pltpu.with_memory_space_constraint(a, pltpu.HBM) for a in args])
    sum0, sum1, next0, next1, new0, new1 = pl.pallas_call(
        finish_kernel,
        out_shape=[
            jax.ShapeDtypeStruct((ROWS, WIDE), BF16),
            jax.ShapeDtypeStruct((ROWS, WIDE), BF16),
            jax.ShapeDtypeStruct((RANK, WIDE), F32),
            jax.ShapeDtypeStruct((RANK, WIDE), F32),
            jax.ShapeDtypeStruct((ROWS, WIDE), F32),
            jax.ShapeDtypeStruct((ROWS, WIDE), F32),
        ],
        in_specs=[vmem] * 4,
        out_specs=[hbm] * 6,
        scratch_shapes=[
            pltpu.VMEM((2, ROWS, WIDE), BF16),
            pltpu.VMEM((2, RANK, WIDE), F32),
            dma((10,)),
        ],
        name="finish",
        compiler_params=pltpu.CompilerParams(vmem_limit_bytes=8 << 20),
    )(*held)
    return sum0, sum1, next0.T, next1.T, new0[None], new1[None]


def solution(mesh):
    wide = P("dp", None, "tensor")
    tall = P("tensor", None)
    flat = P(None, "tensor")
    return jax.shard_map(
        shards,
        mesh=mesh,
        in_specs=(wide, wide, wide, wide, tall, tall),
        out_specs=(flat, flat, tall, tall, wide, wide),
        check_vma=False,
    )
```

```python
import functools

import jax
import jax.numpy as jnp
from jax import lax
from jax.experimental import pallas as pl
from jax.experimental.pallas import tpu as pltpu
from jax.sharding import PartitionSpec as P

MESH = pl.DeviceIdType.MESH
F32, BF16 = jnp.float32, jnp.bfloat16
HIGHEST = lax.Precision.HIGHEST
NX, NY, NZ = 4, 4, 8
ROWS, RANK, WIDE = 256, 32, 1792
CH = 256
NCH = WIDE // CH
BARE = 4
NN = (((1,), (0,)), ((), ()))
NT = (((1,), (1,)), ((), ()))
TN = (((0,), (0,)), ((), ()))


def split(value):
    high = value.astype(BF16)
    low = (value - high.astype(F32)).astype(BF16)
    return high, low


def product(a, b, dims):
    return lax.dot_general(a, b, dims, preferred_element_type=F32)


def triple(value):
    high, low = split(value)
    return jnp.concatenate([high, low, high], axis=0)


def inverse_factors(gram0, gram1):
    row = lax.broadcasted_iota(jnp.int32, (8, 128), 0)
    lane = lax.broadcasted_iota(jnp.int32, (8, 128), 1)
    first = lane < 64

    def spread(value, shape=(8, 128)):
        return jnp.broadcast_to(value, shape)

    def column(i, j):
        rows = slice(8 * i, 8 * i + 8)
        return jnp.where(first, spread(gram0[rows, j : j + 1]), spread(gram1[rows, j : j + 1]))

    parts = RANK // 8
    columns = [[column(i, j) if i >= j // 8 else None for i in range(parts)] for j in range(RANK)]
    unit = [jnp.where((lane == row + 8 * i) | (lane == row + 8 * i + 64), 1.0, 0.0) for i in range(parts)]
    pivots = [jnp.ones((8, 128), F32) for _ in range(parts)]
    for j in range(RANK):
        at, sub = j // 8, j % 8
        now = columns[j]
        pivot = spread(now[at][sub : sub + 1])
        pivots[at] = jnp.where(row == sub, pivot, pivots[at])
        if j == RANK - 1:
            break
        scale = 1.0 / pivot
        factor = [now[i] * scale if i >= at else None for i in range(parts)]
        factor[at] = jnp.where(row > sub, factor[at], 0.0)
        for k in range(j + 1, RANK):
            entry = spread(now[k // 8][k % 8 : k % 8 + 1])
            for i in range(k // 8, parts):
                columns[k][i] = columns[k][i] - factor[i] * entry
        entry = spread(unit[at][sub : sub + 1])
        for i in range(at, parts):
            unit[i] = unit[i] - factor[i] * entry
    both = jnp.concatenate([unit[i] * lax.rsqrt(pivots[i]) for i in range(parts)], axis=0)
    return both[:, :RANK], both[:, 64 : 64 + RANK]


def main_kernel(
    grad0, grad1, error0, error1, q0, q1,
    tsum, wide, new0, new1,
    graw, full, qv, fhi, flo, psend, precv, zbuf, lmine, left,
    tbuf, xr, zs, zr,
    ldg, lde, ldq, s1, r1, s3, r3, s4, r4,
    sx, rx, sz, rz, sgz, rgz, sgx, rgx,
):
    grads, errors, qs = (grad0, grad1), (error0, error1), (q0, q1)
    news = (new0, new1)
    dp, tensor = lax.axis_index("dp"), lax.axis_index("tensor")
    z, x = lax.div(dp, NX), lax.rem(dp, NX)
    y, c = lax.div(tensor, 2), lax.rem(tensor, 2)

    def device(dz=0, dx=0, dy=0, dc=0):
        return (
            lax.rem(z + dz, NZ) * NX + lax.rem(x + dx, NX),
            lax.rem(y + dy, NY) * 2 + lax.rem(c + dc, 2),
        )

    def send(src, dst, send_sem, recv_sem, to):
        pltpu.make_async_remote_copy(
            src_ref=src, dst_ref=dst, send_sem=send_sem, recv_sem=recv_sem,
            device_id=to, device_id_type=MESH,
        ).start()

    def wait(ref, sem):
        pltpu.make_async_copy(ref, ref, sem).wait()

    groups = [(0, 0, 4), (0, 4, 7), (1, 0, 5), (1, 5, 7)]

    def load(number):
        b, low, high = groups[number]
        cols = pl.ds(low * CH, (high - low) * CH)
        pltpu.make_async_copy(errors[b].at[0, :, cols], full.at[b, :, cols], lde.at[number]).start()
        pltpu.make_async_copy(grads[b].at[0, :, cols], graw.at[b, :, cols], ldg.at[number]).start()

    pltpu.make_async_copy(qs[0], qv.at[0], ldq.at[0]).start()
    for number in range(3):
        load(number)
    pltpu.make_async_copy(qs[1], qv.at[1], ldq.at[1]).start()

    barrier = pltpu.get_barrier_semaphore()
    plane = [(dx, dy) for dx in range(NX) for dy in range(NY) if (dx, dy) != (0, 0)]
    plane.sort(key=lambda d: -(min(d[0], NX - d[0]) + min(d[1], NY - d[1])))
    column = (4, 3, 5, 2, 6, 1, 7)
    peers = [device(dx=dx, dy=dy) for dx, dy in plane]
    peers += [device(dc=1)] + [device(dz=k, dc=dc) for k in column for dc in range(2)]
    for peer in peers:
        pl.semaphore_signal(barrier, inc=1, device_id=peer, device_id_type=MESH)

    for number, (b, low, high) in enumerate(groups):
        if low == 0:
            wait(qv.at[b], ldq.at[b])
            qhi, qlo = split(qv[b])
            both = jnp.concatenate([qhi, qlo], axis=0)
            acc, rest_acc = jnp.zeros((ROWS, 2 * RANK), F32), jnp.zeros((ROWS, RANK), F32)
        cols = pl.ds(low * CH, (high - low) * CH)
        wait(full.at[b, :, cols], lde.at[number])
        wait(graw.at[b, :, cols], ldg.at[number])
        if number + 3 < len(groups):
            load(number + 3)
        for j in range(low, high):
            cols = slice(j * CH, (j + 1) * CH)
            value = graw[b, :, cols].astype(F32) + full[b, :, cols]
            top, rest = split(value)
            full[b, :, cols], fhi[b, :, cols], flo[b, :, cols] = value, top, rest
            acc += product(top, both[:, cols], NT)
            rest_acc += product(rest, qhi[:, cols], NT)
        if high < NCH:
            continue
        acc = (acc[:, :RANK] + acc[:, RANK:] + rest_acc).T
        for k in range(8):
            psend[8 * b + k] = acc[8 * (k // 2) : 8 * (k // 2) + 8, 128 * (k % 2) : 128 * (k % 2) + 128]
        if b == 0:
            pl.semaphore_wait(barrier, len(peers))
        for xo in (2 * b, 2 * b + 1):
            for dy in (2, 1, 3, 0):

                def give(xo=xo, dy=dy):
                    yo = lax.rem(y + dy, NY)
                    slot = lax.rem(xo - x + NX, NX) * NY + dy - 1
                    to = (z * NX + xo, yo * 2 + c)
                    send(psend.at[xo * NY + yo], precv.at[slot], s1, r1, to)

                if dy:
                    give()
                else:
                    pl.when(x != xo)(give)

    mine = x * NY + y
    wait(precv, r1)
    part = psend[mine]
    for k in range(15):
        part += precv[k]
    zbuf[0] = part
    for k in column:
        for dc in (1, 0):
            send(zbuf.at[0], zbuf.at[2 * k + dc], s3, r3, device(dz=k, dc=dc))
    send(zbuf.at[0], zbuf.at[1], s3, r3, device(dc=1))
    wait(zbuf.at[pl.ds(1, 15)], r3)
    part = zbuf[2 * z + c]
    for k in range(1, 2 * NZ):
        part += zbuf[2 * lax.rem(z - k // 2 + NZ, NZ) + lax.rem(c + k, 2)]
    lmine[...] = part
    for dx, dy in plane:
        send(lmine, left.at[mine], s4, r4.at[lax.div(x, 2)], device(dx=dx, dy=dy))
    pltpu.make_async_copy(lmine, left.at[mine], r4.at[lax.div(x, 2)]).start()

    skip = lax.rem(BARE - z + NZ, NZ)
    skip = lax.div(skip, 4) * 2 * (skip - 4) + (1 - lax.div(skip, 4)) * (7 - 2 * skip)
    order = []
    for k in range(NCH):
        i = k + lax.div(k - skip + NZ, NZ)
        away = lax.rem(4 + (1 - 2 * lax.rem(i, 2)) * lax.div(i + 1, 2), NZ)
        order.append((lax.rem(z + away + NZ - 1 - BARE, NZ), away))
    owned = lax.rem(z + NZ - 1 - BARE, NZ)

    lefts = []
    for b in range(2):
        wait(left.at[pl.ds(8 * b, 8)], r4.at[b])
        rows = [jnp.concatenate([left[8 * b + 2 * k], left[8 * b + 2 * k + 1]], axis=1) for k in range(4)]
        lefts.append(jnp.concatenate(rows, axis=0))
        lhi, llo = split(lefts[b])
        both = jnp.concatenate([lhi, llo], axis=0)
        for run in ((0,), (1, 2, 3), (4, 5, 6)):
            for k in run:
                chunk = order[k][0]
                cols = pl.ds(pl.multiple_of(chunk * CH, CH), CH)
                first = product(both, fhi[b, :, cols], NN)
                value = first[:RANK] + first[RANK:] + product(lhi, flo[b, :, cols], NN)
                tbuf[chunk, b] = value.reshape(NX, 8, CH)
            for k in run:
                chunk = order[k][0]
                for dx in (2, 1, 3):
                    src = tbuf.at[chunk, b, lax.rem(x + dx, NX)]
                    send(src, xr.at[chunk, b, dx - 1], sx, rx.at[b, chunk], device(dx=dx))

    for b in range(2):
        for k, (chunk, away) in enumerate(order):
            wait(xr.at[chunk, b], rx.at[b, chunk])
            zs[b, chunk] = tbuf[chunk, b, x] + xr[chunk, b, 0] + xr[chunk, b, 1] + xr[chunk, b, 2]

            def pass_on(b=b, k=k, chunk=chunk, away=away):
                send(zs.at[b, chunk], zr.at[b, away], sz.at[b, k // 6], rz.at[b], device(dz=away))

            if k < NCH - 1:
                pass_on()
            else:
                pl.when(z == BARE)(pass_on)

    grams = [
        lax.dot_general(a, a, NT, precision=HIGHEST, preferred_element_type=F32) for a in lefts
    ]
    inverses = inverse_factors(*grams)
    for b in range(2):
        ortho = lax.dot_general(inverses[b], lefts[b], NN, precision=HIGHEST, preferred_element_type=F32)
        weight = lax.dot_general(inverses[b], ortho, TN, precision=HIGHEST, preferred_element_type=F32)
        weight = jnp.concatenate([weight, inverses[b].T], axis=1)
        top = weight.astype(BF16).astype(F32)
        wide[b] = jnp.concatenate([top, top, weight - top], axis=0).T.astype(BF16)

    for b in range(2):

        if b == 1:
            for e in range(2):
                for j in range(NCH):
                    own = tbuf[j, e].reshape(RANK, CH)
                    cols = slice(j * CH, (j + 1) * CH)
                    news[e][:, cols] = full[e, :, cols] - product(wide[e, :ROWS], triple(own), NN)

        @pl.when(z != BARE)
        def _():
            wait(zr.at[b, pl.ds(1, 7)], rz.at[b])
            part = zs[b, owned]
            for k in range(1, NZ):
                part += zr[b, k]
            tsum[owned, b, x] = part
            here = tsum.at[owned, b, x]
            for place in (0, 1, 2, 3, 7, 6, 5, 4):

                @pl.when(z != place)
                def _():
                    to = (place * NX + x, tensor)
                    send(here, here, sgz.at[b], rgz.at[b, owned], to)

            for dx in (2, 1, 3):
                send(here, here, sgx, rgx, device(dx=dx))

    wait(precv, s1)
    wait(zbuf.at[pl.ds(1, 15)], s3)
    wait(precv, s4)
    wait(xr, sx)
    for b in range(2):
        wait(zs.at[b, pl.ds(0, 6)], sz.at[b, 0])

        @pl.when(z == BARE)
        def _():
            wait(zs.at[b, 0], sz.at[b, 1])

        @pl.when(z != BARE)
        def _():
            wait(zr.at[b, pl.ds(1, 7)], sgz.at[b])

    for b in range(2):
        for k in reversed(range(NCH)):

            def forward(b=b, chunk=order[k][0]):
                here = tsum.at[chunk, b, x]
                wait(here, rgz.at[b, chunk])
                for dx in (2, 1, 3):
                    send(here, here, sgx, rgx, device(dx=dx))

            if k < NCH - 1:
                forward()
            else:
                pl.when(z == BARE)(forward)

    wait(xr, rgx)

    wait(xr, sgx)


def finish_kernel(
    tsum, wide, new0, new1, sum0, sum1, next0, next1, out0, out1, sums, nexts, sem
):
    copies = [pltpu.make_async_copy(new0, out0, sem.at[0]), pltpu.make_async_copy(new1, out1, sem.at[1])]
    for copy in copies:
        copy.start()
    for low, high in ((0, 4), (4, 7)):
        for b in range(2):
            for j in range(low, high):
                cols = slice(j * CH, (j + 1) * CH)
                value = product(wide[b], triple(tsum[j, b].reshape(RANK, CH)), NN)
                sums[b, :, cols] = value[:ROWS].astype(BF16)
                nexts[b, :, cols] = value[ROWS:]
            cols = pl.ds(low * CH, (high - low) * CH)
            for held, out in ((sums, (sum0, sum1)), (nexts, (next0, next1))):
                copy = pltpu.make_async_copy(held.at[b, :, cols], out[b].at[:, cols], sem.at[len(copies)])
                copy.start()
                copies.append(copy)
    for copy in copies:
        copy.wait()


def shards(grad0, grad1, error0, error1, q0, q1):
    args = (grad0, grad1, error0, error1, q0.T, q1.T)
    vmem = pl.BlockSpec(memory_space=pltpu.VMEM)
    hbm = pl.BlockSpec(memory_space=pltpu.HBM)
    dma = pltpu.SemaphoreType.DMA
    scratch = [
        pltpu.VMEM((2, ROWS, WIDE), BF16),
        pltpu.VMEM((2, ROWS, WIDE), F32),
        pltpu.VMEM((2, RANK, WIDE), F32),
        pltpu.VMEM((2, ROWS, WIDE), BF16),
        pltpu.VMEM((2, ROWS, WIDE), BF16),
        pltpu.VMEM((16, 8, 128), F32),
        pltpu.VMEM((15, 8, 128), F32),
        pltpu.VMEM((2 * NZ, 8, 128), F32),
        pltpu.VMEM((8, 128), F32),
        pltpu.VMEM((16, 8, 128), F32),
        pltpu.VMEM((NCH, 2, NX, 8, CH), F32),
        pltpu.VMEM((NCH, 2, NX - 1, 8, CH), F32),
        pltpu.VMEM((2, NCH, 8, CH), F32),
        pltpu.VMEM((2, NZ, 8, CH), F32),
        dma((4,)), dma((4,)), dma((2,)),
        dma, dma, dma, dma, dma, dma((2,)),
        dma, dma((2, NCH)), dma((2, 2)), dma((2,)),
        dma((2,)), dma((2, NCH)), dma, dma,
    ]
    held = pl.pallas_call(
        main_kernel,
        out_shape=[
            pltpu.VMEM((NCH, 2, NX, 8, CH), F32),
            pltpu.VMEM((2, ROWS + RANK, 3 * RANK), BF16),
            pltpu.VMEM((ROWS, WIDE), F32),
            pltpu.VMEM((ROWS, WIDE), F32),
        ],
        in_specs=[hbm] * 6,
        out_specs=[vmem] * 4,
        scratch_shapes=scratch,
        name="compress",
        compiler_params=pltpu.CompilerParams(
            collective_id=0, has_side_effects=True, vmem_limit_bytes=36 << 20
        ),
    )(*[pltpu.with_memory_space_constraint(a, pltpu.HBM) for a in args])
    sum0, sum1, next0, next1, new0, new1 = pl.pallas_call(
        finish_kernel,
        out_shape=[
            jax.ShapeDtypeStruct((ROWS, WIDE), BF16),
            jax.ShapeDtypeStruct((ROWS, WIDE), BF16),
            jax.ShapeDtypeStruct((RANK, WIDE), F32),
            jax.ShapeDtypeStruct((RANK, WIDE), F32),
            jax.ShapeDtypeStruct((ROWS, WIDE), F32),
            jax.ShapeDtypeStruct((ROWS, WIDE), F32),
        ],
        in_specs=[vmem] * 4,
        out_specs=[hbm] * 6,
        scratch_shapes=[
            pltpu.VMEM((2, ROWS, WIDE), BF16),
            pltpu.VMEM((2, RANK, WIDE), F32),
            dma((10,)),
        ],
        name="finish",
        compiler_params=pltpu.CompilerParams(vmem_limit_bytes=8 << 20),
    )(*held)
    return sum0, sum1, next0.T, next1.T, new0[None], new1[None]


def solution(mesh):
    wide = P("dp", None, "tensor")
    tall = P("tensor", None)
    flat = P(None, "tensor")
    return jax.shard_map(
        shards,
        mesh=mesh,
        in_specs=(wide, wide, wide, wide, tall, tall),
        out_specs=(flat, flat, tall, tall, wide, wide),
        check_vma=False,
    )
```
